32 devices in a mesh: expert: 8 (over z, y), etp: 4 (over x, core).
Axes of the slice: x: 2, y: 2, z: 4, core: 2. Of those that a mesh axis runs over, the one named last changes fastest.
Arguments:
- tokens: bfloat16 [1024, 4096], P('expert', 'etp'), may hold values from -6 to 6
- expert_ids: int32 [1024, 8], P('expert'), may hold values from 0 to 15, all different within a row; in each aligned block of 128 rows (0 to 127, 128 to 255, ...) at most 96 rows name the same one
- gate_probs: float32 [1024, 8], P('expert'), may hold values from 0.1 to 0.5
- w_gate: bfloat16 [16, 1536, 4096], P('expert', 'etp'), may hold values from -0.09375 to 0.09375
- w_up: bfloat16 [16, 1536, 4096], P('expert', 'etp'), may hold values from -0.09375 to 0.09375
- w_down: bfloat16 [16, 1536, 4096], P('expert', None, 'etp'), may hold values from -0.15625 to 0.15625
Outputs:
- moe_out: bfloat16 [1024, 4096], P('expert', 'etp')
The draws below stay inside these ranges and needn't reach their ends.
Inputs may be any that keep to these rules, and one draw needn't show every extreme that they name: `expert_ids`: within each aligned block of 128 token rows (the rows of one index of expert), no expert is named by more than 96 rows, a bound that some block reaches; the 8 experts of a row differ.
All inputs are finite; a program needn't handle non-finite values.
Results may differ from the reference program's by a relative error of at most 0.0058.
Values may be sent and summed in bfloat16 or wider, within the bound.
A program may use at most 128 MiB of HBM per device.

```python
import math
import jax
import jax.numpy as jnp
import numpy as np
from jax import lax

D = 4096
FF = 1536
TOPK = 8
TOK_DEV = 128
TOKENS = 1024
EXPERTS = 16
CAP = 96
N_EXPERT = 8


def level_of(rng, extent, pieces, least, top_value):
    gain = 1.0
    for axis_at, shards_of in pieces:
        steps = jax.random.uniform(jax.random.fold_in(jax.random.fold_in(rng, 6), axis_at), (shards_of,), jnp.float32, least / len(pieces), top_value / len(pieces))
        gain = gain * jnp.repeat(jnp.exp(steps), extent[axis_at] // shards_of).reshape((-1,) + (1,) * (len(extent) - 1 - axis_at))
    return gain


def assign_block(stream_key, own, number, rows, count, top, limit, slope):
    order = jax.random.permutation(stream_key, count)
    packed, usual = load_shares(count, rows * top, limit, slope, True), load_shares(count, rows * top, limit, slope, False)
    places = jnp.arange(count)

    def named(lengths, turn):
        used = int((lengths > 0).sum())
        fixed = max(1, used // 4)
        moved = fixed + (places - fixed + turn * (used - fixed)) % max(1, count - fixed)
        return jnp.zeros((count,), jnp.int32).at[order[jnp.where(places < fixed, places, moved)]].set(jnp.asarray(lengths, jnp.int32))

    lengths = jnp.where(number % 4 == 0, named(packed, number // 4), named(usual, number - number // 4 - 1))
    mixed = jax.random.permutation(jax.random.fold_in(own, 3), count)
    donor, receiver = mixed[0:count // 2 * 2:2], mixed[1:count // 2 * 2:2]
    margin = jnp.minimum(lengths[donor] - 1, limit - lengths[receiver]) // 2
    margin = jnp.where((donor == order[0]) | (receiver == order[0]) | (lengths[receiver] == 0), 0, jnp.maximum(margin, 0))
    moved = jax.random.randint(jax.random.fold_in(own, 4), (count // 2,), 0, 1 << 20) % (margin + 1)
    lengths = lengths.at[donor].add(-moved).at[receiver].add(moved)
    items = jnp.searchsorted(jnp.cumsum(lengths), jnp.arange(rows * top), side="right").astype(jnp.int32)
    grid = items.reshape(top, rows).T
    grid = grid[jax.random.permutation(jax.random.fold_in(own, 1), rows)]
    turn = jax.random.randint(jax.random.fold_in(own, 2), (rows, 1), 0, top)
    return jnp.take_along_axis(grid, (jnp.arange(top)[None, :] + turn) % top, axis=1)


def load_shares(number_of, total, reach, slope, full):
    loads = [(1 << 20) // math.isqrt(standing ** slope) + 1 for standing in range(1, number_of + 1)]
    largest = reach if full else min(reach, max(-(-total // number_of), total * loads[0] // sum(loads)))
    least = 1 if total - largest >= number_of - 1 else 0
    given, rest = [largest] + [least] * (number_of - 1), total - largest - least * (number_of - 1)
    while rest > 0:
        free = [i for i in range(1, number_of) if given[i] < largest] or [i for i in range(1, number_of) if given[i] < reach]
        mass, budget = sum([loads[i] for i in free]), rest
        for i in free:
            addition = min(reach - given[i], max(1, budget * loads[i] // mass), rest)
            given[i] = given[i] + addition
            rest = rest - addition
    return np.array(given)


def noise(own_key, dims, spread, limit, shards=(), kind=jnp.bfloat16):
    values = spread * jax.random.normal(own_key, dims, jnp.float32)
    if shards:
        values = values * level_of(own_key, dims, shards, -0.22, 0.18)
    return jnp.clip(values, -limit, limit).astype(kind)


def setup_inputs(seed: int = 0) -> dict:
    keys = jax.random.split(jax.random.key(seed), 7)
    tokens = noise(keys[0], (TOKENS, D), 1.0, 6.0, ((0, 8), (1, 4)))
    expert_ids_keys = jax.random.split(jax.random.fold_in(keys[1], 1), TOKENS // TOK_DEV)
    expert_ids_turns = jax.random.permutation(jax.random.fold_in(keys[1], 3), TOKENS // TOK_DEV)
    expert_ids = jax.vmap(lambda own, number: assign_block(jax.random.fold_in(keys[1], 2), own, number, TOK_DEV, EXPERTS, TOPK, CAP, 2))(expert_ids_keys, expert_ids_turns).reshape((TOKENS, TOPK))
    gate_probs = jnp.clip(0.1 + 0.4 * jax.random.uniform(keys[2], (TOKENS, TOPK), jnp.float32) ** level_of(keys[2], (TOKENS, TOPK), ((0, 8),), -0.2, 0.2), 0.1, 0.5)
    w_gate = noise(keys[3], (EXPERTS, FF, D), D ** -0.5, 0.09375, ((0, 8), (1, 4)))
    w_up = noise(keys[4], (EXPERTS, FF, D), D ** -0.5, 0.09375, ((0, 8), (1, 4)))
    w_down = noise(keys[5], (EXPERTS, FF, D), FF ** -0.5, 0.15625, ((0, 8), (2, 4)))
    return {"tokens": tokens, "expert_ids": expert_ids, "gate_probs": gate_probs, "w_gate": w_gate, "w_up": w_up, "w_down": w_down}


def reference(tokens, expert_ids, gate_probs, w_gate, w_up, w_down):
    blocks = N_EXPERT
    per_block = TOK_DEV * TOPK
    pairs = expert_ids.reshape(blocks, per_block)
    onehot = (pairs[:, :, None] == jnp.arange(EXPERTS, dtype=jnp.int32)[None, None, :]).astype(jnp.int32)
    position = jnp.sum(jnp.cumsum(onehot, axis=1) * onehot, axis=2) - 1
    block_index = jnp.arange(blocks, dtype=jnp.int32)[:, None]
    slot_index = ((pairs * blocks + block_index) * CAP + position).reshape(-1).astype(jnp.int32)
    total_slots = EXPERTS * blocks * CAP
    token_of = (jnp.arange(TOKENS * TOPK, dtype=jnp.int32) // TOPK).astype(jnp.int32)
    source_row = jnp.full((total_slots,), TOKENS, jnp.int32).at[slot_index].set(token_of)
    padded = jnp.concatenate([tokens, jnp.zeros((1, D), tokens.dtype)], axis=0)

    def one_expert(which):
        start = (which * blocks * CAP).astype(jnp.int32)
        rows_here = lax.dynamic_slice_in_dim(source_row, start, blocks * CAP)
        inputs = padded[rows_here]
        gate = lax.dot_general(inputs, w_gate[which], (((1,), (1,)), ((), ())), preferred_element_type=jnp.float32)
        upper = lax.dot_general(inputs, w_up[which], (((1,), (1,)), ((), ())), preferred_element_type=jnp.float32)
        hidden = (jax.nn.silu(gate) * upper).astype(jnp.bfloat16)
        return jnp.dot(hidden, w_down[which], preferred_element_type=jnp.float32).astype(jnp.bfloat16)

    results = lax.map(one_expert, jnp.arange(EXPERTS, dtype=jnp.int32))
    results = results.reshape(total_slots, D)
    picked = results[slot_index].astype(jnp.float32).reshape(TOKENS, TOPK, D)
    mixed = jnp.sum(picked * gate_probs[:, :, None], axis=1)
    return mixed.astype(jnp.bfloat16)
```

```python
import functools
import jax
import jax.numpy as jnp
from jax import lax
from jax.experimental import pallas as pl
from jax.experimental.pallas import tpu as pltpu
from jax.sharding import PartitionSpec as P

MESH = pl.DeviceIdType.MESH
VMEM_BUDGET = 60 * 2**20
PAIR = 2


def routed(tokens, expert_ids, gate_probs, w_gate, w_up, w_down):
    tok_rows = tokens.shape[0]
    top_count = expert_ids.shape[1]
    owners = lax.axis_size("expert")
    local_experts = w_gate.shape[0]
    expert_count = owners * local_experts
    capacity = 3 * tok_rows * top_count // (2 * expert_count)
    pairs = expert_ids.reshape(-1)
    onehot = (pairs[:, None] == jnp.arange(expert_count, dtype=jnp.int32)[None, :]).astype(
        jnp.int32
    )
    position = jnp.sum(jnp.cumsum(onehot, axis=0) * onehot, axis=1) - 1
    slot_index = pairs * capacity + position
    token_of = jnp.arange(pairs.shape[0], dtype=jnp.int32) // top_count
    source_row = (
        jnp.full((expert_count * capacity,), tok_rows, jnp.int32).at[slot_index].set(token_of)
    )
    padded = jnp.concatenate([tokens, jnp.zeros((1, tokens.shape[1]), tokens.dtype)], axis=0)
    outgoing = padded[source_row].reshape(owners, local_experts, capacity, tokens.shape[1])
    full_rows = lax.all_gather(
        lax.all_to_all(outgoing, "expert", split_axis=0, concat_axis=0, tiled=True),
        "etp",
        axis=3,
        tiled=True,
    )
    gate = jnp.einsum("sjcd,jfd->sjcf", full_rows, w_gate, preferred_element_type=jnp.float32)
    upper = jnp.einsum("sjcd,jfd->sjcf", full_rows, w_up, preferred_element_type=jnp.float32)
    hidden = (jax.nn.silu(gate) * upper).astype(jnp.bfloat16)
    hidden_all = lax.all_gather(hidden, "etp", axis=3, tiled=True)
    result = jnp.einsum("sjcf,jfd->sjcd", hidden_all, w_down, preferred_element_type=jnp.float32)
    returned = lax.all_to_all(
        result.astype(jnp.bfloat16), "expert", split_axis=0, concat_axis=0, tiled=True
    )
    results = returned.reshape(expert_count * capacity, returned.shape[3])
    picked = results[slot_index].astype(jnp.float32) * gate_probs.reshape(-1)[:, None]
    mixed = jnp.sum(picked.reshape(tok_rows, top_count, results.shape[1]), axis=1)
    return mixed.astype(jnp.bfloat16)


def fused_kernel(
    owners, splits,
    own_ref, ids_ref, probs_ref, wg_hbm, wu_hbm, wd_hbm,
    out_ref,
    tok, wg, wu, wd, hid, share, acc, ysend, yrecv, zsend, zrecv,
    w_sem, send_sem, tok_sem, share_sem, hid_sem, y_sem, z_sem,
):
    rows, cols = own_ref.shape
    local_experts, units = wg_hbm.shape[0], wg_hbm.shape[1]
    ny = PAIR
    nz = owners // ny
    me, part = lax.axis_index("expert"), lax.axis_index("etp")
    z, y = me // ny, me % ny
    other_y = 1 - y
    x, core = part // PAIR, part % PAIR
    part_x = (1 - x) * PAIR + core
    part_sib = x * PAIR + (1 - core)
    part_sib_x = (1 - x) * PAIR + (1 - core)
    dev_x, dev_sib, dev_y = (me, part_x), (me, part_sib), (z * ny + other_y, part)

    loads = [
        pltpu.make_async_copy(src, dst, w_sem.at[i])
        for i, (src, dst) in enumerate(((wg_hbm, wg), (wu_hbm, wu), (wd_hbm, wd)))
    ]
    for load in loads:
        load.start()

    barrier = pltpu.get_barrier_semaphore()
    peers = [(lax.rem(me + k, owners), part) for k in range(1, owners)] + [dev_x, dev_sib]
    for peer in peers:
        pl.semaphore_signal(barrier, inc=1, device_id=peer, device_id_type=MESH)

    ids, probs = ids_ref[...], probs_ref[...]
    for e in range(owners * local_experts):
        share[me, e : e + 1, :] = jnp.sum(
            jnp.where(ids == e, probs, 0.0), axis=0, keepdims=True
        )

    pl.semaphore_wait(barrier, len(peers))

    sends = []

    def send(src, dst, arrived, device):
        copy = pltpu.make_async_remote_copy(
            src_ref=src, dst_ref=dst, send_sem=send_sem.at[len(sends)], recv_sem=arrived,
            device_id=device, device_id_type=MESH,
        )
        copy.start()
        sends.append(copy)

    def await_arrival(dst, arrived):
        pltpu.make_async_remote_copy(
            src_ref=dst, dst_ref=dst, send_sem=send_sem.at[0], recv_sem=arrived,
            device_id=dev_sib, device_id_type=MESH,
        ).wait_recv()

    def tok_at(s, t):
        return tok.at[
            pl.ds(pl.multiple_of(s * rows, rows), rows), pl.ds(pl.multiple_of(t * cols, cols), cols)
        ]

    def send_tok(s, t, device, src=None):
        block = tok_at(s, t)
        send(block if src is None else src, block, tok_sem.at[s, t], device)

    def await_tok(s, t):
        await_arrival(tok_at(s, t), tok_sem.at[s, t])

    def z_of(k):
        return lax.rem(z - k + nz, nz)

    z_peers = [(lax.rem(z + k, nz) * ny + y, part) for k in range(1, nz)]
    send_tok(me, part, dev_x, own_ref)
    send_tok(me, part, dev_y, own_ref)
    for peer in z_peers:
        send_tok(me, part, peer, own_ref)
    send_tok(me, part, dev_sib, own_ref)
    for peer in peers[: owners - 1]:
        send(share.at[me], share.at[me], share_sem.at[me], peer)
    tok[
        pl.ds(pl.multiple_of(me * rows, rows), rows), pl.ds(pl.multiple_of(part * cols, cols), cols)
    ] = own_ref[...]
    await_tok(me, part_x)
    send_tok(me, part_x, dev_y)
    for peer in z_peers:
        send_tok(me, part_x, peer)
    send_tok(me, part_x, dev_sib)

    def forward_z(k):
        s = z_of(k) * ny + y
        for t in (part, part_x):
            await_tok(s, t)
            send_tok(s, t, dev_y)
            send_tok(s, t, dev_sib)

    def finish_tokens(k):
        mine, other = z_of(k) * ny + y, z_of(k) * ny + other_y
        for t in (part, part_x):
            await_tok(other, t)
            send_tok(other, t, dev_sib)
        for s in (mine, other):
            for t in (part_sib, part_sib_x):
                await_tok(s, t)

    group = ny * rows

    def group_rows(k):
        return pl.ds(pl.multiple_of(z_of(k) * group, group), group)

    def hid_at(k, t):
        return hid.at[:, group_rows(k), pl.ds(pl.multiple_of(t * units, units), units)]

    nt = (((1,), (1,)), ((), ()))

    def gate_up(k):
        for j in range(local_experts):
            inputs = tok[group_rows(k), :]
            gate = lax.dot_general(inputs, wg[j], nt, preferred_element_type=jnp.float32)
            upper = lax.dot_general(inputs, wu[j], nt, preferred_element_type=jnp.float32)
            hid[j, group_rows(k), pl.ds(pl.multiple_of(part * units, units), units)] = (
                gate / (1.0 + jnp.exp(-gate)) * upper
            ).astype(jnp.bfloat16)
        for device in (dev_x, dev_sib):
            send(hid_at(k, part), hid_at(k, part), hid_sem.at[z_of(k), part], device)

    def finish_hidden(k):
        await_arrival(hid_at(k, part_x), hid_sem.at[z_of(k), part_x])
        send(hid_at(k, part_x), hid_at(k, part_x), hid_sem.at[z_of(k), part_x], dev_sib)
        for t in (part_sib, part_sib_x):
            await_arrival(hid_at(k, t), hid_sem.at[z_of(k), t])

    diagonal = lax.broadcasted_iota(jnp.int32, (rows, rows), 0) == lax.broadcasted_iota(
        jnp.int32, (rows, rows), 1
    )

    def down(k):
        for j in range(local_experts):
            result = jnp.dot(hid[j, group_rows(k), :], wd[j], preferred_element_type=jnp.float32)
            for i in range(ny):
                line = share[z_of(k) * ny + i, pl.ds(me * local_experts + j, 1), :]
                column = jnp.sum(
                    jnp.where(diagonal, jnp.broadcast_to(line, (rows, rows)), 0.0),
                    axis=1, keepdims=True,
                )
                term = result[i * rows : (i + 1) * rows] * column
                if j == 0:
                    acc[k, i] = term
                else:
                    acc[k, i] += term
        ysend[k] = acc[k, other_y].astype(jnp.bfloat16)
        send(ysend.at[k], yrecv.at[k], y_sem.at[k], dev_y)

    def reduce_y(k):
        await_arrival(yrecv.at[k], y_sem.at[k])
        total = acc[k, y] + yrecv[k].astype(jnp.float32)
        if k == 0:
            acc[0, y] = total
        else:
            zsend[k] = total.astype(jnp.bfloat16)
            send(zsend.at[k], zrecv.at[k], z_sem.at[k], (z_of(k) * ny + y, part))

    if nz > 1:
        forward_z(1)
    for k in range(nz):
        finish_tokens(k)
        if k == 0:
            loads[0].wait()
            loads[1].wait()
        gate_up(k)
        if k > 0:
            reduce_y(k - 1)
        if k + 2 < nz:
            forward_z(k + 2)
        if k == 0:
            loads[2].wait()
            for i in range(1, owners):
                s = lax.rem(me + i, owners)
                await_arrival(share.at[s], share_sem.at[s])
        finish_hidden(k)
        down(k)
    reduce_y(nz - 1)
    total = acc[0, y]
    for k in range(1, nz):
        await_arrival(zrecv.at[k], z_sem.at[k])
        total = total + zrecv[k].astype(jnp.float32)
    out_ref[...] = total.astype(jnp.bfloat16)
    for copy in sends:
        copy.wait_send()


def fused(owners, splits, tokens, expert_ids, gate_probs, w_gate, w_up, w_down):
    rows, cols = tokens.shape
    local_experts, units, width = w_gate.shape
    nz = owners // PAIR
    everything = owners * rows
    bf16, f32 = jnp.bfloat16, jnp.float32
    vmem = pl.BlockSpec(memory_space=pltpu.VMEM)
    hbm = pl.BlockSpec(memory_space=pl.ANY)
    dma = pltpu.SemaphoreType.DMA
    count = 2 * (nz + 2) + (owners - 1) + 4 * (nz - 1) + 2 * nz + 3 * nz + nz + nz
    flops = 6 * everything * local_experts * units * width
    return pl.pallas_call(
        functools.partial(fused_kernel, owners, splits),
        out_shape=jax.ShapeDtypeStruct((rows, cols), bf16),
        in_specs=[vmem, vmem, vmem, hbm, hbm, hbm],
        out_specs=vmem,
        scratch_shapes=[
            pltpu.VMEM((everything, width), bf16),
            pltpu.VMEM(w_gate.shape, bf16),
            pltpu.VMEM(w_up.shape, bf16),
            pltpu.VMEM(w_down.shape, bf16),
            pltpu.VMEM((local_experts, everything, w_down.shape[1]), bf16),
            pltpu.VMEM((owners, owners * local_experts, rows), f32),
            pltpu.VMEM((nz, PAIR, rows, cols), f32),
            pltpu.VMEM((nz, rows, cols), bf16),
            pltpu.VMEM((nz, rows, cols), bf16),
            pltpu.VMEM((nz, rows, cols), bf16),
            pltpu.VMEM((nz, rows, cols), bf16),
            dma((3,)),
            dma((count,)),
            dma((owners, splits)),
            dma((owners,)),
            dma((nz, splits)),
            dma((nz,)),
            dma((nz,)),
        ],
        compiler_params=pltpu.CompilerParams(
            collective_id=0, has_side_effects=True, vmem_limit_bytes=VMEM_BUDGET
        ),
        cost_estimate=pl.CostEstimate(
            flops=flops, bytes_accessed=6 * w_gate.size, transcendentals=0
        ),
        name="moe",
    )(tokens, expert_ids.T, gate_probs.T, w_gate, w_up, w_down)


def on_device(owners, splits, tokens, expert_ids, gate_probs, w_gate, w_up, w_down):
    rows, cols = tokens.shape
    local_experts, units, width = w_gate.shape
    everything = owners * rows
    need = 2 * (everything * width + 3 * w_gate.size + local_experts * everything * units * splits)
    need += owners * rows * cols * 8 + 6 * rows * local_experts * width
    fits = need <= VMEM_BUDGET and rows % 128 == 0 and cols % 128 == 0 and units % 128 == 0
    if fits and splits == PAIR * PAIR and owners % PAIR == 0:
        return fused(owners, splits, tokens, expert_ids, gate_probs, w_gate, w_up, w_down)
    return routed(tokens, expert_ids, gate_probs, w_gate, w_up, w_down)


def solution(mesh):
    return jax.shard_map(
        functools.partial(on_device, mesh.shape["expert"], mesh.shape["etp"]),
        mesh=mesh,
        in_specs=(
            P("expert", "etp"),
            P("expert", None),
            P("expert", None),
            P("expert", "etp", None),
            P("expert", "etp", None),
            P("expert", None, "etp"),
        ),
        out_specs=P("expert", "etp"),
        check_vma=False,
    )
```

```python
import functools
import jax
import jax.numpy as jnp
from jax import lax
from jax.experimental import pallas as pl
from jax.experimental.pallas import tpu as pltpu
from jax.sharding import PartitionSpec as P

MESH = pl.DeviceIdType.MESH
VMEM_BUDGET = 60 * 2**20
PAIR = 2


def routed(tokens, expert_ids, gate_probs, w_gate, w_up, w_down):
    tok_rows = tokens.shape[0]
    top_count = expert_ids.shape[1]
    owners = lax.axis_size("expert")
    local_experts = w_gate.shape[0]
    expert_count = owners * local_experts
    capacity = 3 * tok_rows * top_count // (2 * expert_count)
    pairs = expert_ids.reshape(-1)
    onehot = (pairs[:, None] == jnp.arange(expert_count, dtype=jnp.int32)[None, :]).astype(
        jnp.int32
    )
    position = jnp.sum(jnp.cumsum(onehot, axis=0) * onehot, axis=1) - 1
    slot_index = pairs * capacity + position
    token_of = jnp.arange(pairs.shape[0], dtype=jnp.int32) // top_count
    source_row = (
        jnp.full((expert_count * capacity,), tok_rows, jnp.int32).at[slot_index].set(token_of)
    )
    padded = jnp.concatenate([tokens, jnp.zeros((1, tokens.shape[1]), tokens.dtype)], axis=0)
    outgoing = padded[source_row].reshape(owners, local_experts, capacity, tokens.shape[1])
    full_rows = lax.all_gather(
        lax.all_to_all(outgoing, "expert", split_axis=0, concat_axis=0, tiled=True),
        "etp",
        axis=3,
        tiled=True,
    )
    gate = jnp.einsum("sjcd,jfd->sjcf", full_rows, w_gate, preferred_element_type=jnp.float32)
    upper = jnp.einsum("sjcd,jfd->sjcf", full_rows, w_up, preferred_element_type=jnp.float32)
    hidden = (jax.nn.silu(gate) * upper).astype(jnp.bfloat16)
    hidden_all = lax.all_gather(hidden, "etp", axis=3, tiled=True)
    result = jnp.einsum("sjcf,jfd->sjcd", hidden_all, w_down, preferred_element_type=jnp.float32)
    returned = lax.all_to_all(
        result.astype(jnp.bfloat16), "expert", split_axis=0, concat_axis=0, tiled=True
    )
    results = returned.reshape(expert_count * capacity, returned.shape[3])
    picked = results[slot_index].astype(jnp.float32) * gate_probs.reshape(-1)[:, None]
    mixed = jnp.sum(picked.reshape(tok_rows, top_count, results.shape[1]), axis=1)
    return mixed.astype(jnp.bfloat16)


def fused_kernel(
    owners, splits,
    own_ref, ids_ref, probs_ref, wg_hbm, wu_hbm, wd_hbm,
    out_ref,
    tok, turned, wg, wu, wd, hid, share, acc, ysend, yrecv, zsend, zrecv,
    w_sem, send_sem, tok_sem, share_sem, hid_sem, y_sem, z_sem,
):
    rows, cols = own_ref.shape
    local_experts, units = wg_hbm.shape[0], wg_hbm.shape[1]
    ny = PAIR
    nz = owners // ny
    me, part = lax.axis_index("expert"), lax.axis_index("etp")
    z, y = me // ny, me % ny
    other_y = 1 - y
    x, core = part // PAIR, part % PAIR
    part_x = (1 - x) * PAIR + core
    part_sib = x * PAIR + (1 - core)
    part_sib_x = (1 - x) * PAIR + (1 - core)
    dev_x, dev_sib, dev_y = (me, part_x), (me, part_sib), (z * ny + other_y, part)

    loads = [
        pltpu.make_async_copy(src, dst, w_sem.at[i])
        for i, (src, dst) in enumerate(((wg_hbm, wg), (wu_hbm, wu), (wd_hbm, wd)))
    ]
    for load in loads:
        load.start()

    barrier = pltpu.get_barrier_semaphore()
    peers = [(lax.rem(me + k, owners), part) for k in range(1, owners)] + [dev_x, dev_sib]
    for peer in peers:
        pl.semaphore_signal(barrier, inc=1, device_id=peer, device_id_type=MESH)

    ids, probs = ids_ref[...], probs_ref[...]
    for e in range(owners * local_experts):
        share[me, e : e + 1, :] = jnp.sum(
            jnp.where(ids == e, probs, 0.0), axis=0, keepdims=True
        )

    pl.semaphore_wait(barrier, len(peers))

    sends = []

    def send(make, device, allowed=None):
        index = len(sends)

        def copy():
            src, dst, arrived = make()
            return pltpu.make_async_remote_copy(
                src_ref=src, dst_ref=dst, send_sem=send_sem.at[index], recv_sem=arrived,
                device_id=device, device_id_type=MESH,
            )

        def when(action):
            if allowed is None:
                action()
            else:
                pl.when(allowed)(action)

        when(lambda: copy().start())
        sends.append(lambda: when(lambda: copy().wait_send()))

    def await_arrival(dst, arrived):
        pltpu.make_async_remote_copy(
            src_ref=dst, dst_ref=dst, send_sem=send_sem.at[0], recv_sem=arrived,
            device_id=dev_sib, device_id_type=MESH,
        ).wait_recv()

    def tok_at(s, t):
        return tok.at[
            pl.ds(pl.multiple_of(s * rows, rows), rows), pl.ds(pl.multiple_of(t * cols, cols), cols)
        ]

    def send_tok(s, t, device, src=None, allowed=None):
        def make():
            block = tok_at(s, t)
            return (block if src is None else src), block, tok_sem.at[s, t]

        send(make, device, allowed)

    def await_tok(s, t):
        await_arrival(tok_at(s, t), tok_sem.at[s, t])

    upper_half = z * 2 // nz
    mirrored = z + upper_half * (nz - 1 - 2 * z)

    def z_of(k):
        near = (2 * mirrored - k + nz) // nz
        step = -((k + 1) // 2) if k % 2 else k // 2
        g = near * (mirrored + step) + (1 - near) * k
        return g + upper_half * (nz - 1 - 2 * g)

    def z_neighbour(z_next):
        return (z_next * ny + y, part), (z_next >= 0) & (z_next < nz)

    z_sides = [z_neighbour(z + 1), z_neighbour(z - 1)]
    send_tok(me, part, dev_x, own_ref)
    send_tok(me, part, dev_y, own_ref)
    for device, there in z_sides:
        send_tok(me, part, device, own_ref, there)
    send_tok(me, part, dev_sib, own_ref)
    for peer in peers[: owners - 1]:
        send(lambda: (share.at[me], share.at[me], share_sem.at[me]), peer)
    tok[
        pl.ds(pl.multiple_of(me * rows, rows), rows), pl.ds(pl.multiple_of(part * cols, cols), cols)
    ] = own_ref[...]
    await_tok(me, part_x)
    send_tok(me, part_x, dev_y)
    for device, there in z_sides:
        send_tok(me, part_x, device, None, there)
    send_tok(me, part_x, dev_sib)

    def forward_z(k):
        s = z_of(k) * ny + y
        from_below = (z - z_of(k) + nz - 1) // nz
        device, there = z_neighbour(z - 1 + 2 * from_below)
        for t in (part, part_x):
            await_tok(s, t)
            send_tok(s, t, device, None, there)
            send_tok(s, t, dev_y)
            send_tok(s, t, dev_sib)

    def finish_tokens(k):
        mine, other = z_of(k) * ny + y, z_of(k) * ny + other_y
        for t in (part, part_x):
            await_tok(other, t)
            send_tok(other, t, dev_sib)
        for s in (mine, other):
            for t in (part_sib, part_sib_x):
                await_tok(s, t)

    group = ny * rows

    def group_rows(k):
        return pl.ds(pl.multiple_of(z_of(k) * group, group), group)

    def hid_at(k, j, t):
        return hid.at[j, group_rows(k), pl.ds(pl.multiple_of(t * units, units), units)]

    def send_hid(k, j, t, device):
        send(lambda: (hid_at(k, j, t), hid_at(k, j, t), hid_sem.at[z_of(k), t, j]), device)

    def gate_up(k):
        for i in range(splits):
            turned[i * cols : (i + 1) * cols, :] = tok[
                group_rows(k), i * cols : (i + 1) * cols
            ].T
        for j in range(local_experts):
            gate = jnp.dot(wg[j], turned[...], preferred_element_type=jnp.float32)
            upper = jnp.dot(wu[j], turned[...], preferred_element_type=jnp.float32)
            mixed = gate / (1.0 + jnp.exp(-gate)) * upper
            hid[j, group_rows(k), pl.ds(pl.multiple_of(part * units, units), units)] = (
                mixed.T.astype(jnp.bfloat16)
            )
            for device in (dev_x, dev_sib):
                send_hid(k, j, part, device)

    def finish_hidden(k, j):
        await_arrival(hid_at(k, j, part_x), hid_sem.at[z_of(k), part_x, j])
        send_hid(k, j, part_x, dev_sib)
        for t in (part_sib, part_sib_x):
            await_arrival(hid_at(k, j, t), hid_sem.at[z_of(k), t, j])

    diagonal = lax.broadcasted_iota(jnp.int32, (rows, rows), 0) == lax.broadcasted_iota(
        jnp.int32, (rows, rows), 1
    )

    def down(k):
        for j in range(local_experts):
            finish_hidden(k, j)
            result = jnp.dot(hid[j, group_rows(k), :], wd[j], preferred_element_type=jnp.float32)
            for i in range(ny):
                line = share[z_of(k) * ny + i, pl.ds(me * local_experts + j, 1), :]
                column = jnp.sum(
                    jnp.where(diagonal, jnp.broadcast_to(line, (rows, rows)), 0.0),
                    axis=1, keepdims=True,
                )
                term = result[i * rows : (i + 1) * rows] * column
                if j == 0:
                    acc[k, i] = term
                else:
                    acc[k, i] += term
        ysend[k] = acc[k, other_y].astype(jnp.bfloat16)
        send(lambda: (ysend.at[k], yrecv.at[k], y_sem.at[k]), dev_y)

    def reduce_y(k):
        await_arrival(yrecv.at[k], y_sem.at[k])
        total = acc[k, y] + yrecv[k].astype(jnp.float32)
        if k == 0:
            acc[0, y] = total
        else:
            zsend[k] = total.astype(jnp.bfloat16)
            send(lambda: (zsend.at[k], zrecv.at[z], z_sem.at[z]), (z_of(k) * ny + y, part))

    if nz > 1:
        forward_z(1)
    for k in range(nz):
        finish_tokens(k)
        if k == 0:
            loads[0].wait()
            loads[1].wait()
        gate_up(k)
        if k > 0:
            reduce_y(k - 1)
        if k + 2 < nz:
            forward_z(k + 2)
        if k == 0:
            loads[2].wait()
            for i in range(1, owners):
                s = lax.rem(me + i, owners)
                await_arrival(share.at[s], share_sem.at[s])
        down(k)
    reduce_y(nz - 1)
    total = acc[0, y]
    for k in range(1, nz):
        source = lax.rem(z + k, nz)
        await_arrival(zrecv.at[source], z_sem.at[source])
        total = total + zrecv[source].astype(jnp.float32)
    out_ref[...] = total.astype(jnp.bfloat16)
    for wait in sends:
        wait()


def fused(owners, splits, tokens, expert_ids, gate_probs, w_gate, w_up, w_down):
    rows, cols = tokens.shape
    local_experts, units, width = w_gate.shape
    nz = owners // PAIR
    everything = owners * rows
    bf16, f32 = jnp.bfloat16, jnp.float32
    vmem = pl.BlockSpec(memory_space=pltpu.VMEM)
    hbm = pl.BlockSpec(memory_space=pl.ANY)
    dma = pltpu.SemaphoreType.DMA
    count = 9 + (owners - 1) + 6 * (nz - 1) + 2 * nz + 3 * local_experts * nz + 2 * nz
    flops = 6 * everything * local_experts * units * width
    return pl.pallas_call(
        functools.partial(fused_kernel, owners, splits),
        out_shape=jax.ShapeDtypeStruct((rows, cols), bf16),
        in_specs=[vmem, vmem, vmem, hbm, hbm, hbm],
        out_specs=vmem,
        scratch_shapes=[
            pltpu.VMEM((everything, width), bf16),
            pltpu.VMEM((width, PAIR * rows), bf16),
            pltpu.VMEM(w_gate.shape, bf16),
            pltpu.VMEM(w_up.shape, bf16),
            pltpu.VMEM(w_down.shape, bf16),
            pltpu.VMEM((local_experts, everything, w_down.shape[1]), bf16),
            pltpu.VMEM((owners, owners * local_experts, rows), f32),
            pltpu.VMEM((nz, PAIR, rows, cols), f32),
            pltpu.VMEM((nz, rows, cols), bf16),
            pltpu.VMEM((nz, rows, cols), bf16),
            pltpu.VMEM((nz, rows, cols), bf16),
            pltpu.VMEM((nz, rows, cols), bf16),
            dma((3,)),
            dma((count,)),
            dma((owners, splits)),
            dma((owners,)),
            dma((nz, splits, local_experts)),
            dma((nz,)),
            dma((nz,)),
        ],
        compiler_params=pltpu.CompilerParams(
            collective_id=0, has_side_effects=True, vmem_limit_bytes=VMEM_BUDGET
        ),
        cost_estimate=pl.CostEstimate(
            flops=flops, bytes_accessed=6 * w_gate.size, transcendentals=0
        ),
        name="moe",
    )(tokens, expert_ids.T, gate_probs.T, w_gate, w_up, w_down)


def on_device(owners, splits, tokens, expert_ids, gate_probs, w_gate, w_up, w_down):
    rows, cols = tokens.shape
    local_experts, units, width = w_gate.shape
    everything = owners * rows
    need = 2 * (everything * width + 3 * w_gate.size + local_experts * everything * units * splits)
    need += owners * rows * cols * 8 + 4 * rows * width + 6 * rows * local_experts * width
    fits = need <= VMEM_BUDGET and rows % 128 == 0 and cols % 128 == 0 and units % 128 == 0
    if fits and splits == PAIR * PAIR and owners % PAIR == 0:
        return fused(owners, splits, tokens, expert_ids, gate_probs, w_gate, w_up, w_down)
    return routed(tokens, expert_ids, gate_probs, w_gate, w_up, w_down)


def solution(mesh):
    return jax.shard_map(
        functools.partial(on_device, mesh.shape["expert"], mesh.shape["etp"]),
        mesh=mesh,
        in_specs=(
            P("expert", "etp"),
            P("expert", None),
            P("expert", None),
            P("expert", "etp", None),
            P("expert", "etp", None),
            P("expert", None, "etp"),
        ),
        out_specs=P("expert", "etp"),
        check_vma=False,
    )
```

```python
import functools
import jax
import jax.numpy as jnp
from jax import lax
from jax.experimental import pallas as pl
from jax.experimental.pallas import tpu as pltpu
from jax.sharding import PartitionSpec as P

MESH = pl.DeviceIdType.MESH
VMEM_BUDGET = 60 * 2**20
PAIR = 2


def routed(tokens, expert_ids, gate_probs, w_gate, w_up, w_down):
    tok_rows = tokens.shape[0]
    top_count = expert_ids.shape[1]
    owners = lax.axis_size("expert")
    local_experts = w_gate.shape[0]
    expert_count = owners * local_experts
    capacity = 3 * tok_rows * top_count // (2 * expert_count)
    pairs = expert_ids.reshape(-1)
    onehot = (pairs[:, None] == jnp.arange(expert_count, dtype=jnp.int32)[None, :]).astype(
        jnp.int32
    )
    position = jnp.sum(jnp.cumsum(onehot, axis=0) * onehot, axis=1) - 1
    slot_index = pairs * capacity + position
    token_of = jnp.arange(pairs.shape[0], dtype=jnp.int32) // top_count
    source_row = (
        jnp.full((expert_count * capacity,), tok_rows, jnp.int32).at[slot_index].set(token_of)
    )
    padded = jnp.concatenate([tokens, jnp.zeros((1, tokens.shape[1]), tokens.dtype)], axis=0)
    outgoing = padded[source_row].reshape(owners, local_experts, capacity, tokens.shape[1])
    full_rows = lax.all_gather(
        lax.all_to_all(outgoing, "expert", split_axis=0, concat_axis=0, tiled=True),
        "etp",
        axis=3,
        tiled=True,
    )
    gate = jnp.einsum("sjcd,jfd->sjcf", full_rows, w_gate, preferred_element_type=jnp.float32)
    upper = jnp.einsum("sjcd,jfd->sjcf", full_rows, w_up, preferred_element_type=jnp.float32)
    hidden = (jax.nn.silu(gate) * upper).astype(jnp.bfloat16)
    hidden_all = lax.all_gather(hidden, "etp", axis=3, tiled=True)
    result = jnp.einsum("sjcf,jfd->sjcd", hidden_all, w_down, preferred_element_type=jnp.float32)
    returned = lax.all_to_all(
        result.astype(jnp.bfloat16), "expert", split_axis=0, concat_axis=0, tiled=True
    )
    results = returned.reshape(expert_count * capacity, returned.shape[3])
    picked = results[slot_index].astype(jnp.float32) * gate_probs.reshape(-1)[:, None]
    mixed = jnp.sum(picked.reshape(tok_rows, top_count, results.shape[1]), axis=1)
    return mixed.astype(jnp.bfloat16)


def fused_kernel(
    owners, splits,
    own_ref, ids_ref, probs_ref, wg_hbm, wu_hbm, wd_hbm,
    out_ref,
    tok, turned, wg, wu, wd, hid, share, acc, ysend, yrecv, zsend, zrecv,
    w_sem, send_sem, tok_sem, share_sem, hid_sem, y_sem, z_sem,
):
    rows, cols = own_ref.shape
    local_experts, units = wg_hbm.shape[0], wg_hbm.shape[1]
    ny = PAIR
    nz = owners // ny
    me, part = lax.axis_index("expert"), lax.axis_index("etp")
    z, y = me // ny, me % ny
    other_y = 1 - y
    x, core = part // PAIR, part % PAIR
    part_x = (1 - x) * PAIR + core
    part_sib = x * PAIR + (1 - core)
    part_sib_x = (1 - x) * PAIR + (1 - core)
    dev_x, dev_sib, dev_y = (me, part_x), (me, part_sib), (z * ny + other_y, part)

    loads = [
        pltpu.make_async_copy(src, dst, w_sem.at[i])
        for i, (src, dst) in enumerate(((wg_hbm, wg), (wu_hbm, wu), (wd_hbm, wd)))
    ]
    for load in loads:
        load.start()

    barrier = pltpu.get_barrier_semaphore()
    peers = [(lax.rem(me + k, owners), part) for k in range(1, owners)] + [dev_x, dev_sib]
    for peer in peers:
        pl.semaphore_signal(barrier, inc=1, device_id=peer, device_id_type=MESH)

    ids, probs = ids_ref[...], probs_ref[...]
    for e in range(owners * local_experts):
        share[me, e : e + 1, :] = jnp.sum(
            jnp.where(ids == e, probs, 0.0), axis=0, keepdims=True
        )

    pl.semaphore_wait(barrier, len(peers))

    sends = []

    def send(make, device, allowed=None):
        index = len(sends)

        def copy():
            src, dst, arrived = make()
            return pltpu.make_async_remote_copy(
                src_ref=src, dst_ref=dst, send_sem=send_sem.at[index], recv_sem=arrived,
                device_id=device, device_id_type=MESH,
            )

        def when(action):
            if allowed is None:
                action()
            else:
                pl.when(allowed)(action)

        when(lambda: copy().start())
        sends.append(lambda: when(lambda: copy().wait_send()))

    def await_arrival(dst, arrived):
        pltpu.make_async_remote_copy(
            src_ref=dst, dst_ref=dst, send_sem=send_sem.at[0], recv_sem=arrived,
            device_id=dev_sib, device_id_type=MESH,
        ).wait_recv()

    first = rows * 5 // 8 // 16 * 16
    spans = ((0, first), (first, rows - first))

    def tok_at(s, t, h):
        start, size = spans[h]
        return tok.at[
            pl.ds(pl.multiple_of(s * rows + start, 16), size),
            pl.ds(pl.multiple_of(t * cols, cols), cols),
        ]

    def send_tok(s, t, h, device, own=False, allowed=None):
        def make():
            block = tok_at(s, t, h)
            return (own_ref.at[pl.ds(*spans[h]), :] if own else block), block, tok_sem.at[s, t, h]

        send(make, device, allowed)

    def await_tok(s, t, h):
        await_arrival(tok_at(s, t, h), tok_sem.at[s, t, h])

    upper_half = z * 2 // nz
    mirrored = z + upper_half * (nz - 1 - 2 * z)

    def z_of(k):
        near = (2 * mirrored - k + nz) // nz
        step = -((k + 1) // 2) if k % 2 else k // 2
        g = near * (mirrored + step) + (1 - near) * k
        return g + upper_half * (nz - 1 - 2 * g)

    def z_neighbour(z_next):
        return (z_next * ny + y, part), (z_next >= 0) & (z_next < nz)

    z_sides = [z_neighbour(z + 1), z_neighbour(z - 1)]
    send_tok(me, part, 0, dev_x, True)
    for h in range(2):
        for device, there in z_sides:
            send_tok(me, part, h, device, True, there)
        send_tok(me, part, h, dev_y, True)
    send_tok(me, part, 1, dev_x, True)
    for h in range(2):
        send_tok(me, part, h, dev_sib, True)
    for peer in peers[: owners - 1]:
        send(lambda: (share.at[me], share.at[me], share_sem.at[me]), peer)
    tok[
        pl.ds(pl.multiple_of(me * rows, rows), rows), pl.ds(pl.multiple_of(part * cols, cols), cols)
    ] = own_ref[...]
    await_tok(me, part_x, 0)
    for device, there in z_sides:
        send_tok(me, part_x, 0, device, False, there)
    send_tok(me, part_x, 0, dev_y)
    send_tok(me, part_x, 0, dev_sib)

    def forward_z(k):
        s = z_of(k) * ny + y
        from_below = (z - z_of(k) + nz - 1) // nz
        device, there = z_neighbour(z - 1 + 2 * from_below)
        for t, h in ((part, 0), (part, 1), (part_x, 0)):
            await_tok(s, t, h)
            send_tok(s, t, h, device, False, there)
            send_tok(s, t, h, dev_y)
            if h == 1:
                send_tok(s, t, h, dev_x)
            send_tok(s, t, h, dev_sib)

    def relay_other(k):
        s = z_of(k) * ny + other_y
        for t, h in ((part, 0), (part, 1), (part_x, 0)):
            await_tok(s, t, h)
            if h == 1:
                send_tok(s, t, h, dev_x)
            send_tok(s, t, h, dev_sib)

    def finish_tokens(k, side):
        s = z_of(k) * ny + side
        await_tok(s, part_x, 1)
        send_tok(s, part_x, 1, dev_sib)
        for t in (part_sib, part_sib_x):
            for h in range(2):
                await_tok(s, t, h)

    def group_rows(k, side):
        if side is None:
            return pl.ds(pl.multiple_of(z_of(k) * ny * rows, rows), ny * rows)
        return pl.ds(pl.multiple_of((z_of(k) * ny + side) * rows, rows), rows)

    def hid_piece(k, side, j, t):
        block = hid.at[
            j, group_rows(k, side), pl.ds(pl.multiple_of(t * units, units), units)
        ]
        return block, hid_sem.at[z_of(k), t, j, 0 if side is None else side]

    def send_hid(k, side, j, t, device):
        def make():
            block, arrived = hid_piece(k, side, j, t)
            return block, block, arrived

        send(make, device)

    def gate_up(k, side=None):
        size = rows if side is not None else ny * rows
        for i in range(splits):
            turned[i * cols : (i + 1) * cols, :size] = tok[
                group_rows(k, side), i * cols : (i + 1) * cols
            ].T
        for j in range(local_experts):
            inputs = turned[:, :size]
            gate = jnp.dot(wg[j], inputs, preferred_element_type=jnp.float32)
            upper = jnp.dot(wu[j], inputs, preferred_element_type=jnp.float32)
            mixed = gate / (1.0 + jnp.exp(-gate)) * upper
            hid[j, group_rows(k, side), pl.ds(pl.multiple_of(part * units, units), units)] = (
                mixed.T.astype(jnp.bfloat16)
            )
            for device in (dev_x, dev_sib):
                send_hid(k, side, j, part, device)

    def finish_hidden(k, side, j):
        await_arrival(*hid_piece(k, side, j, part_x))
        send_hid(k, side, j, part_x, dev_sib)
        for t in (part_sib, part_sib_x):
            await_arrival(*hid_piece(k, side, j, t))

    diagonal = lax.broadcasted_iota(jnp.int32, (rows, rows), 0) == lax.broadcasted_iota(
        jnp.int32, (rows, rows), 1
    )

    def down(k, side=None):
        for j in range(local_experts):
            finish_hidden(k, side, j)
            result = jnp.dot(
                hid[j, group_rows(k, side), :], wd[j], preferred_element_type=jnp.float32
            )
            for i in range(ny if side is None else 1):
                to = i if side is None else side
                line = share[z_of(k) * ny + to, pl.ds(me * local_experts + j, 1), :]
                column = jnp.sum(
                    jnp.where(diagonal, jnp.broadcast_to(line, (rows, rows)), 0.0),
                    axis=1, keepdims=True,
                )
                term = result[i * rows : (i + 1) * rows] * column
                if j == 0:
                    acc[k, to] = term
                else:
                    acc[k, to] += term

    def send_y(k):
        ysend[k] = acc[k, other_y].astype(jnp.bfloat16)
        send(lambda: (ysend.at[k], yrecv.at[k], y_sem.at[k]), dev_y)

    def reduce_y(k):
        await_arrival(yrecv.at[k], y_sem.at[k])
        total = acc[k, y] + yrecv[k].astype(jnp.float32)
        if k == 0:
            acc[0, y] = total
        else:
            zsend[k] = total.astype(jnp.bfloat16)
            send(lambda: (zsend.at[k], zrecv.at[z], z_sem.at[z]), (z_of(k) * ny + y, part))

    last = nz - 1
    forward_z(1)
    relay_other(0)
    for k in range(last):
        finish_tokens(k, y)
        finish_tokens(k, other_y)
        if k == 0:
            loads[0].wait()
            loads[1].wait()
        gate_up(k)
        if k == 0:
            if last > 1:
                forward_z(2)
            loads[2].wait()
            for i in range(1, owners):
                s = lax.rem(me + i, owners)
                await_arrival(share.at[s], share_sem.at[s])
        else:
            reduce_y(k - 1)
        if k + 1 == last:
            finish_tokens(last, y)
            gate_up(last, y)
        relay_other(k + 1)
        down(k)
        send_y(k)
        if k == 0:
            for later in range(3, nz):
                forward_z(later)
    finish_tokens(last, other_y)
    gate_up(last, other_y)
    reduce_y(last - 1)
    down(last, y)
    down(last, other_y)
    send_y(last)
    reduce_y(last)
    total = acc[0, y]
    for k in range(1, nz):
        source = lax.rem(z + k, nz)
        await_arrival(zrecv.at[source], z_sem.at[source])
        total = total + zrecv[source].astype(jnp.float32)
    out_ref[...] = total.astype(jnp.bfloat16)
    for wait in sends:
        wait()


def fused(owners, splits, tokens, expert_ids, gate_probs, w_gate, w_up, w_down):
    rows, cols = tokens.shape
    local_experts, units, width = w_gate.shape
    nz = owners // PAIR
    everything = owners * rows
    bf16, f32 = jnp.bfloat16, jnp.float32
    vmem = pl.BlockSpec(memory_space=pltpu.VMEM)
    hbm = pl.BlockSpec(memory_space=pl.ANY)
    dma = pltpu.SemaphoreType.DMA
    count = 14 + (owners - 1) + 10 * (nz - 1) + 6 * nz + 3 * local_experts * (nz + 1) + 2 * nz
    flops = 6 * everything * local_experts * units * width
    return pl.pallas_call(
        functools.partial(fused_kernel, owners, splits),
        out_shape=jax.ShapeDtypeStruct((rows, cols), bf16),
        in_specs=[vmem, vmem, vmem, hbm, hbm, hbm],
        out_specs=vmem,
        scratch_shapes=[
            pltpu.VMEM((everything, width), bf16),
            pltpu.VMEM((width, PAIR * rows), bf16),
            pltpu.VMEM(w_gate.shape, bf16),
            pltpu.VMEM(w_up.shape, bf16),
            pltpu.VMEM(w_down.shape, bf16),
            pltpu.VMEM((local_experts, everything, w_down.shape[1]), bf16),
            pltpu.VMEM((owners, owners * local_experts, rows), f32),
            pltpu.VMEM((nz, PAIR, rows, cols), f32),
            pltpu.VMEM((nz, rows, cols), bf16),
            pltpu.VMEM((nz, rows, cols), bf16),
            pltpu.VMEM((nz, rows, cols), bf16),
            pltpu.VMEM((nz, rows, cols), bf16),
            dma((3,)),
            dma((count,)),
            dma((owners, splits, 2)),
            dma((owners,)),
            dma((nz, splits, local_experts, PAIR)),
            dma((nz,)),
            dma((nz,)),
        ],
        compiler_params=pltpu.CompilerParams(
            collective_id=0, has_side_effects=True, vmem_limit_bytes=VMEM_BUDGET
        ),
        cost_estimate=pl.CostEstimate(
            flops=flops, bytes_accessed=6 * w_gate.size, transcendentals=0
        ),
        name="moe",
    )(tokens, expert_ids.T, gate_probs.T, w_gate, w_up, w_down)


def on_device(owners, splits, tokens, expert_ids, gate_probs, w_gate, w_up, w_down):
    rows, cols = tokens.shape
    local_experts, units, width = w_gate.shape
    everything = owners * rows
    need = 2 * (everything * width + 3 * w_gate.size + local_experts * everything * units * splits)
    need += owners * rows * cols * 8 + 4 * rows * width + 6 * rows * local_experts * width
    fits = need <= VMEM_BUDGET and rows % 128 == 0 and cols % 128 == 0 and units % 128 == 0
    if fits and splits == PAIR * PAIR and owners % (2 * PAIR) == 0:
        return fused(owners, splits, tokens, expert_ids, gate_probs, w_gate, w_up, w_down)
    return routed(tokens, expert_ids, gate_probs, w_gate, w_up, w_down)


def solution(mesh):
    return jax.shard_map(
        functools.partial(on_device, mesh.shape["expert"], mesh.shape["etp"]),
        mesh=mesh,
        in_specs=(
            P("expert", "etp"),
            P("expert", None),
            P("expert", None),
            P("expert", "etp", None),
            P("expert", "etp", None),
            P("expert", None, "etp"),
        ),
        out_specs=P("expert", "etp"),
        check_vma=False,
    )
```

```python
import functools
import math
import jax
import jax.numpy as jnp
from jax import lax
from jax.experimental import pallas as pl
from jax.experimental.pallas import tpu as pltpu
from jax.sharding import PartitionSpec as P

MESH = pl.DeviceIdType.MESH
VMEM_BUDGET = 60 * 2**20
CHUNK_IN = 512
CHUNK_OUT = 256
PAIR = 2


def routed(tokens, expert_ids, gate_probs, w_gate, w_up, w_down):
    tok_rows = tokens.shape[0]
    top_count = expert_ids.shape[1]
    owners = lax.axis_size("expert")
    local_experts = w_gate.shape[0]
    expert_count = owners * local_experts
    capacity = 3 * tok_rows * top_count // (2 * expert_count)
    pairs = expert_ids.reshape(-1)
    onehot = (pairs[:, None] == jnp.arange(expert_count, dtype=jnp.int32)[None, :]).astype(
        jnp.int32
    )
    position = jnp.sum(jnp.cumsum(onehot, axis=0) * onehot, axis=1) - 1
    slot_index = pairs * capacity + position
    token_of = jnp.arange(pairs.shape[0], dtype=jnp.int32) // top_count
    source_row = (
        jnp.full((expert_count * capacity,), tok_rows, jnp.int32).at[slot_index].set(token_of)
    )
    padded = jnp.concatenate([tokens, jnp.zeros((1, tokens.shape[1]), tokens.dtype)], axis=0)
    outgoing = padded[source_row].reshape(owners, local_experts, capacity, tokens.shape[1])
    full_rows = lax.all_gather(
        lax.all_to_all(outgoing, "expert", split_axis=0, concat_axis=0, tiled=True),
        "etp",
        axis=3,
        tiled=True,
    )
    gate = jnp.einsum("sjcd,jfd->sjcf", full_rows, w_gate, preferred_element_type=jnp.float32)
    upper = jnp.einsum("sjcd,jfd->sjcf", full_rows, w_up, preferred_element_type=jnp.float32)
    hidden = (jax.nn.silu(gate) * upper).astype(jnp.bfloat16)
    hidden_all = lax.all_gather(hidden, "etp", axis=3, tiled=True)
    result = jnp.einsum("sjcf,jfd->sjcd", hidden_all, w_down, preferred_element_type=jnp.float32)
    returned = lax.all_to_all(
        result.astype(jnp.bfloat16), "expert", split_axis=0, concat_axis=0, tiled=True
    )
    results = returned.reshape(expert_count * capacity, returned.shape[3])
    picked = results[slot_index].astype(jnp.float32) * gate_probs.reshape(-1)[:, None]
    mixed = jnp.sum(picked.reshape(tok_rows, top_count, results.shape[1]), axis=1)
    return mixed.astype(jnp.bfloat16)


def fused_kernel(
    owners, splits,
    own_ref, ids_ref, probs_ref, wg_hbm, wu_hbm, wd_hbm,
    out_ref,
    tok, sums, wg, wu, wd, hid, share, acc, ysend, yrecv, zsend, zrecv,
    w_sem, send_sem, tok_sem, share_sem, hid_sem, y_sem, z_sem,
):
    rows, cols = own_ref.shape
    local_experts, units = wg_hbm.shape[0], wg_hbm.shape[1]
    ny = PAIR
    nz = owners // ny
    me, part = lax.axis_index("expert"), lax.axis_index("etp")
    z, y = me // ny, me % ny
    other_y = 1 - y
    x, core = part // PAIR, part % PAIR
    part_x = (1 - x) * PAIR + core
    part_sib = x * PAIR + (1 - core)
    part_sib_x = (1 - x) * PAIR + (1 - core)
    dev_x, dev_sib, dev_y = (me, part_x), (me, part_sib), (z * ny + other_y, part)

    loads = [
        pltpu.make_async_copy(src, dst, w_sem.at[i])
        for i, (src, dst) in enumerate(((wg_hbm, wg), (wu_hbm, wu), (wd_hbm, wd)))
    ]
    for load in loads:
        load.start()

    barrier = pltpu.get_barrier_semaphore()
    peers = [(lax.rem(me + k, owners), part) for k in range(1, owners)] + [dev_x, dev_sib]
    for peer in peers:
        pl.semaphore_signal(barrier, inc=1, device_id=peer, device_id_type=MESH)

    ids, probs = ids_ref[...], probs_ref[...]
    for e in range(owners * local_experts):
        share[me, e : e + 1, :] = jnp.sum(
            jnp.where(ids == e, probs, 0.0), axis=0, keepdims=True
        )

    pl.semaphore_wait(barrier, len(peers))

    sends = []

    def send(make, device, allowed=None):
        index = len(sends)

        def copy():
            src, dst, arrived = make()
            return pltpu.make_async_remote_copy(
                src_ref=src, dst_ref=dst, send_sem=send_sem.at[index], recv_sem=arrived,
                device_id=device, device_id_type=MESH,
            )

        def when(action):
            if allowed is None:
                action()
            else:
                pl.when(allowed)(action)

        when(lambda: copy().start())
        sends.append(lambda: when(lambda: copy().wait_send()))

    def await_arrival(dst, arrived):
        pltpu.make_async_remote_copy(
            src_ref=dst, dst_ref=dst, send_sem=send_sem.at[0], recv_sem=arrived,
            device_id=dev_sib, device_id_type=MESH,
        ).wait_recv()

    first = rows * 5 // 8 // 16 * 16
    spans = ((0, first), (first, rows - first))

    def tok_at(s, t, h):
        start, size = spans[h]
        return tok.at[
            pl.ds(pl.multiple_of(s * rows + start, 16), size),
            pl.ds(pl.multiple_of(t * cols, cols), cols),
        ]

    def send_tok(s, t, h, device, own=False, allowed=None):
        def make():
            block = tok_at(s, t, h)
            return (own_ref.at[pl.ds(*spans[h]), :] if own else block), block, tok_sem.at[s, t, h]

        send(make, device, allowed)

    def await_tok(s, t, h):
        await_arrival(tok_at(s, t, h), tok_sem.at[s, t, h])

    upper_half = z * 2 // nz
    mirrored = z + upper_half * (nz - 1 - 2 * z)

    def z_of(k):
        near = (2 * mirrored - k + nz) // nz
        step = -((k + 1) // 2) if k % 2 else k // 2
        g = near * (mirrored + step) + (1 - near) * k
        return g + upper_half * (nz - 1 - 2 * g)

    def z_neighbour(z_next):
        return (z_next * ny + y, part), (z_next >= 0) & (z_next < nz)

    z_sides = [z_neighbour(z + 1), z_neighbour(z - 1)]
    send_tok(me, part, 0, dev_x, True)
    for h in range(2):
        for device, there in z_sides:
            send_tok(me, part, h, device, True, there)
        send_tok(me, part, h, dev_y, True)
    send_tok(me, part, 1, dev_x, True)
    for h in range(2):
        send_tok(me, part, h, dev_sib, True)
    for peer in peers[: owners - 1]:
        send(lambda: (share.at[me], share.at[me], share_sem.at[me]), peer)
    tok[
        pl.ds(pl.multiple_of(me * rows, rows), rows), pl.ds(pl.multiple_of(part * cols, cols), cols)
    ] = own_ref[...]
    await_tok(me, part_x, 0)
    for device, there in z_sides:
        send_tok(me, part_x, 0, device, False, there)
    send_tok(me, part_x, 0, dev_y)
    send_tok(me, part_x, 0, dev_sib)

    def forward_z(k):
        s = z_of(k) * ny + y
        from_below = (z - z_of(k) + nz - 1) // nz
        device, there = z_neighbour(z - 1 + 2 * from_below)
        for t, h in ((part, 0), (part, 1), (part_x, 0)):
            await_tok(s, t, h)
            send_tok(s, t, h, device, False, there)
            send_tok(s, t, h, dev_y)
            if h == 1:
                send_tok(s, t, h, dev_x)
            send_tok(s, t, h, dev_sib)

    def relay_other(k):
        s = z_of(k) * ny + other_y
        for t, h in ((part, 0), (part, 1), (part_x, 0)):
            await_tok(s, t, h)
            if h == 1:
                send_tok(s, t, h, dev_x)
            send_tok(s, t, h, dev_sib)

    def finish_tokens(k, side):
        s = z_of(k) * ny + side
        await_tok(s, part_x, 1)
        send_tok(s, part_x, 1, dev_sib)
        for t in (part_sib, part_sib_x):
            for h in range(2):
                await_tok(s, t, h)

    def group_rows(k, side):
        if side is None:
            return pl.ds(pl.multiple_of(z_of(k) * ny * rows, rows), ny * rows)
        return pl.ds(pl.multiple_of((z_of(k) * ny + side) * rows, rows), rows)

    def hid_piece(k, side, j, t):
        block = hid.at[
            j, group_rows(k, side), pl.ds(pl.multiple_of(t * units, units), units)
        ]
        return block, hid_sem.at[z_of(k), t, j, 0 if side is None else side]

    def send_hid(k, side, j, t, device):
        def make():
            block, arrived = hid_piece(k, side, j, t)
            return block, block, arrived

        send(make, device)

    width = tok.shape[1]
    step_in = math.gcd(width, CHUNK_IN)

    def gate_up(k, side=None):
        size = rows if side is not None else ny * rows
        sums[:, :, :size] = jnp.zeros((2 * local_experts, units, size), jnp.float32)

        def add(i, carry):
            features = pl.ds(pl.multiple_of(i * step_in, step_in), step_in)
            turned = tok[group_rows(k, side), features].T
            for j in range(local_experts):
                for m, w in enumerate((wg, wu)):
                    sums[2 * j + m, :, :size] += jnp.dot(
                        w[j, :, features], turned, preferred_element_type=jnp.float32
                    )
            return carry

        lax.fori_loop(0, width // step_in, add, 0)
        for j in range(local_experts):
            gate = sums[2 * j, :, :size]
            mixed = gate / (1.0 + jnp.exp(-gate)) * sums[2 * j + 1, :, :size]
            hid[j, group_rows(k, side), pl.ds(pl.multiple_of(part * units, units), units)] = (
                mixed.T.astype(jnp.bfloat16)
            )
            for device in (dev_x, dev_sib):
                send_hid(k, side, j, part, device)

    def finish_hidden(k, side, j):
        await_arrival(*hid_piece(k, side, j, part_x))
        send_hid(k, side, j, part_x, dev_sib)
        for t in (part_sib, part_sib_x):
            await_arrival(*hid_piece(k, side, j, t))

    diagonal = lax.broadcasted_iota(jnp.int32, (rows, rows), 0) == lax.broadcasted_iota(
        jnp.int32, (rows, rows), 1
    )

    step_out = math.gcd(cols, CHUNK_OUT)

    def down(k, side=None):
        places = range(ny) if side is None else (side,)
        weights = []
        for j in range(local_experts):
            finish_hidden(k, side, j)
            for to in places:
                line = share[z_of(k) * ny + to, pl.ds(me * local_experts + j, 1), :]
                weights.append(
                    jnp.sum(
                        jnp.where(diagonal, jnp.broadcast_to(line, (rows, rows)), 0.0),
                        axis=1, keepdims=True,
                    )
                )

        def column_block(i, carry):
            block = pl.ds(pl.multiple_of(i * step_out, step_out), step_out)
            totals = [0.0] * len(places)
            for j in range(local_experts):
                result = jnp.dot(
                    hid[j, group_rows(k, side), :], wd[j, :, block],
                    preferred_element_type=jnp.float32,
                )
                for p in range(len(places)):
                    totals[p] += (
                        result[p * rows : (p + 1) * rows] * weights[j * len(places) + p]
                    )
            for p, to in enumerate(places):
                acc[k, to, :, block] = totals[p]
            return carry

        lax.fori_loop(0, cols // step_out, column_block, 0)

    def send_y(k):
        ysend[k] = acc[k, other_y].astype(jnp.bfloat16)
        send(lambda: (ysend.at[k], yrecv.at[k], y_sem.at[k]), dev_y)

    def reduce_y(k):
        await_arrival(yrecv.at[k], y_sem.at[k])
        total = acc[k, y] + yrecv[k].astype(jnp.float32)
        if k == 0:
            acc[0, y] = total
        else:
            zsend[k] = total.astype(jnp.bfloat16)
            send(lambda: (zsend.at[k], zrecv.at[z], z_sem.at[z]), (z_of(k) * ny + y, part))

    last = nz - 1
    forward_z(1)
    relay_other(0)
    for k in range(last):
        finish_tokens(k, y)
        finish_tokens(k, other_y)
        if k == 0:
            loads[0].wait()
            loads[1].wait()
        gate_up(k)
        if k == 0:
            if last > 1:
                forward_z(2)
            loads[2].wait()
            for i in range(1, owners):
                s = lax.rem(me + i, owners)
                await_arrival(share.at[s], share_sem.at[s])
        else:
            reduce_y(k - 1)
        if k + 1 == last:
            finish_tokens(last, y)
            gate_up(last, y)
        relay_other(k + 1)
        down(k)
        send_y(k)
        if k == 0:
            for later in range(3, nz):
                forward_z(later)
    finish_tokens(last, other_y)
    gate_up(last, other_y)
    reduce_y(last - 1)
    down(last, y)
    down(last, other_y)
    send_y(last)
    reduce_y(last)
    total = acc[0, y]
    for k in range(1, nz):
        source = lax.rem(z + k, nz)
        await_arrival(zrecv.at[source], z_sem.at[source])
        total = total + zrecv[source].astype(jnp.float32)
    out_ref[...] = total.astype(jnp.bfloat16)
    for wait in sends:
        wait()


def fused(owners, splits, tokens, expert_ids, gate_probs, w_gate, w_up, w_down):
    rows, cols = tokens.shape
    local_experts, units, width = w_gate.shape
    nz = owners // PAIR
    everything = owners * rows
    bf16, f32 = jnp.bfloat16, jnp.float32
    vmem = pl.BlockSpec(memory_space=pltpu.VMEM)
    hbm = pl.BlockSpec(memory_space=pl.ANY)
    dma = pltpu.SemaphoreType.DMA
    count = 14 + (owners - 1) + 10 * (nz - 1) + 6 * nz + 3 * local_experts * (nz + 1) + 2 * nz
    flops = 6 * everything * local_experts * units * width
    return pl.pallas_call(
        functools.partial(fused_kernel, owners, splits),
        out_shape=jax.ShapeDtypeStruct((rows, cols), bf16),
        in_specs=[vmem, vmem, vmem, hbm, hbm, hbm],
        out_specs=vmem,
        scratch_shapes=[
            pltpu.VMEM((everything, width), bf16),
            pltpu.VMEM((2 * local_experts, units, PAIR * rows), f32),
            pltpu.VMEM(w_gate.shape, bf16),
            pltpu.VMEM(w_up.shape, bf16),
            pltpu.VMEM(w_down.shape, bf16),
            pltpu.VMEM((local_experts, everything, w_down.shape[1]), bf16),
            pltpu.VMEM((owners, owners * local_experts, rows), f32),
            pltpu.VMEM((nz, PAIR, rows, cols), f32),
            pltpu.VMEM((nz, rows, cols), bf16),
            pltpu.VMEM((nz, rows, cols), bf16),
            pltpu.VMEM((nz, rows, cols), bf16),
            pltpu.VMEM((nz, rows, cols), bf16),
            dma((3,)),
            dma((count,)),
            dma((owners, splits, 2)),
            dma((owners,)),
            dma((nz, splits, local_experts, PAIR)),
            dma((nz,)),
            dma((nz,)),
        ],
        compiler_params=pltpu.CompilerParams(
            collective_id=0, has_side_effects=True, vmem_limit_bytes=VMEM_BUDGET
        ),
        cost_estimate=pl.CostEstimate(
            flops=flops, bytes_accessed=6 * w_gate.size, transcendentals=0
        ),
        name="moe",
    )(tokens, expert_ids.T, gate_probs.T, w_gate, w_up, w_down)


def on_device(owners, splits, tokens, expert_ids, gate_probs, w_gate, w_up, w_down):
    rows, cols = tokens.shape
    local_experts, units, width = w_gate.shape
    everything = owners * rows
    need = 2 * (everything * width + 3 * w_gate.size + local_experts * everything * units * splits)
    need += owners * rows * cols * 8 + 16 * local_experts * units * rows + 6 * rows * local_experts * width
    fits = need <= VMEM_BUDGET and rows % 128 == 0 and cols % 128 == 0 and units % 128 == 0
    if fits and splits == PAIR * PAIR and owners % (2 * PAIR) == 0:
        return fused(owners, splits, tokens, expert_ids, gate_probs, w_gate, w_up, w_down)
    return routed(tokens, expert_ids, gate_probs, w_gate, w_up, w_down)


def solution(mesh):
    return jax.shard_map(
        functools.partial(on_device, mesh.shape["expert"], mesh.shape["etp"]),
        mesh=mesh,
        in_specs=(
            P("expert", "etp"),
            P("expert", None),
            P("expert", None),
            P("expert", "etp", None),
            P("expert", "etp", None),
            P("expert", None, "etp"),
        ),
        out_specs=P("expert", "etp"),
        check_vma=False,
    )
```
